128 devices in a mesh: sec: 8 (over x_lo, y), col: 16 (over x_hi, z, core).
Axes of the slice: x: 4 (x_hi: 2, x_lo: 2; x = x_hi * 2 + x_lo), y: 4, z: 4, core: 2. Of those that a mesh axis runs over, the one named last changes fastest.
Arguments:
- matrix_rows: float32 [8192, 32768], P('sec', 'col'), may hold values from -6 to 6
- factor_bank: float32 [4, 16, 512, 512], P(None, 'sec', 'col'), may hold values from -1 to 1, as said below
- owner_table: int32 [4, 16, 16], P(None, 'sec'), may hold values from 0 to 15, each once within a row
Outputs:
- updated: float32 [8192, 32768], P('sec', 'col')
The draws below stay inside these ranges and needn't reach their ends.
Inputs may be any that keep to these rules, and one draw needn't show every extreme that they name: `factor_bank`: each factor G[r,k] is orthogonal. `owner_table`: for each round and section the list names every row block once.
All inputs are finite; a program needn't handle non-finite values.
Results may differ from the reference program's by a relative error of at most 0.00014.
Values sent between devices are 32-bit elements; how exact they have to be, the bound alone decides.
No kernel may reach another device: no remote copies, remote signals or barrier semaphores. Data moves between devices by JAX's collectives and lax.ppermute only.
A program may use at most 128 MiB of HBM per device.

```python
import jax
import jax.numpy as jnp
from jax import lax

F = 512
ROUNDS = 4
SECTIONS = 16
ROWS = 8192
CUT = 32768
N_COL = 16


def draw_factor_bank(key, part):
    raw = jax.random.normal(key, (ROUNDS, SECTIONS, F, F), jnp.float32)
    orthogonal, upper = jnp.linalg.qr(raw)
    return orthogonal


def level_of(stream_key, shape, split, low, largest):
    loudness, own = 1.0, jax.random.fold_in(stream_key, 6)
    for dim, shards_of in split:
        draws = jnp.exp(jax.random.uniform(jax.random.fold_in(own, dim), (shards_of,), jnp.float32, low / len(split), largest / len(split)))
        loudness = loudness * jnp.repeat(draws, shape[dim] // shards_of).reshape([-1 if axis == dim else 1 for axis in range(len(shape))])
    return loudness


def centred(stream_key, dims, deviation, most, pieces=(), held_as=jnp.bfloat16):
    array = jax.random.normal(stream_key, dims, jnp.float32) * deviation
    if len(pieces) > 0:
        array = level_of(stream_key, dims, pieces, -0.22, 0.18) * array
    return jnp.clip(array, min=-most, max=most).astype(held_as)


def setup_inputs(seed: int = 0) -> dict:
    seeds = jax.random.split(jax.random.key(seed), 4)
    matrix_rows = centred(seeds[0], (ROWS, CUT), 1.0, 6.0, ((0, 8), (1, 16)), jnp.float32)
    factor_bank = draw_factor_bank(jax.random.fold_in(seeds[3], 71), 0)
    owner_table = jax.vmap(lambda own: jax.random.permutation(own, N_COL))(jax.random.split(seeds[2], ROUNDS * SECTIONS)).reshape((ROUNDS, SECTIONS, N_COL)).astype(jnp.int32)
    return {"matrix_rows": matrix_rows, "factor_bank": factor_bank, "owner_table": owner_table}


def assemble(stored, owner_now):
    sections = stored.shape[0]
    extent = stored.shape[1]
    groups = owner_now.shape[1]
    blocks = stored.reshape(sections, groups, extent // groups, extent)
    labels = jnp.arange(groups, dtype=jnp.int32)
    onehot = (owner_now[:, :, None] == labels[None, None, :]).astype(stored.dtype)
    placed = jnp.einsum('scb,scnf->sbnf', onehot, blocks, precision=lax.Precision.HIGHEST)
    return placed.reshape(sections, extent, extent)

def reference(matrix_rows, factor_bank, owner_table):
    current = matrix_rows
    for number in range(ROUNDS):
        factors = assemble(factor_bank[number], owner_table[number])
        if number % 2 == 1:
            current = jnp.roll(current, F // 2, axis=0)
        windows = current.reshape(SECTIONS, F, -1)
        current = lax.map(lambda couple: jnp.dot(couple[0], couple[1], precision=lax.Precision.HIGHEST), (factors, windows))
        current = current.reshape(SECTIONS * F, -1)
        if number % 2 == 1:
            current = jnp.roll(current, -(F // 2), axis=0)
    return current
```

```python
import jax
import jax.numpy as jnp
from jax import lax
from jax.experimental import pallas as pl
from jax.experimental.pallas import tpu as pltpu
from jax.sharding import PartitionSpec as P

F = 512
HALF = 256
TILE = 512
COST = 0.01
CHUNKS = ((0, 512), (512, 1024), (1536, 512))
VMEM = 16 * 1024 * 1024


def shifted(value, steps):
    count = lax.axis_size("sec")
    return lax.ppermute(value, "sec", [(i, (i + steps) % count) for i in range(count)])


def moved(value, target):
    return lax.ppermute(value, "col", [(i, target(i)) for i in range(16)])


def route(h, s):
    return lambda i: ((i // 8) ^ h) * 8 + ((i // 2 + s) % 4) * 2 + i % 2


STEPS = (0, 1, 3, 2)


def on_chip():
    return pl.BlockSpec(memory_space=pltpu.VMEM)


def kernel(body, args, in_specs, out_shapes, out_specs, flops, name, scratch=(), aliases=None):
    moved_bytes = sum(a.size * a.dtype.itemsize for a, b in zip(args, in_specs) if b.memory_space != pltpu.HBM)
    return pl.pallas_call(
        body,
        in_specs=in_specs,
        out_specs=out_specs,
        out_shape=out_shapes,
        scratch_shapes=scratch,
        input_output_aliases=aliases or {},
        compiler_params=pltpu.CompilerParams(vmem_limit_bytes=VMEM),
        cost_estimate=pl.CostEstimate(
            flops=int(COST * flops), bytes_accessed=int(COST * moved_bytes), transcendentals=0
        ),
        name=name,
    )(*args)


def prep(groups, index, owners, name, start=0):
    count = owners.shape[0]

    def body(owner_ref, *refs):
        ins, (hi_ref, lo_ref) = refs[: len(groups)], refs[len(groups) :]
        for array, at, source in index():
            for n in range(count):
                rows = pl.ds(pl.multiple_of(owner_ref[n, source] * 32, 32), 32)
                value = ins[array][at + (start + n,)]
                hi = value.astype(jnp.bfloat16)
                hi_ref[n, rows, :] = hi
                lo_ref[n, rows, :] = (value - hi.astype(jnp.float32)).astype(jnp.bfloat16)

    shape = jax.ShapeDtypeStruct((count, F, F), jnp.bfloat16)
    return kernel(
        body,
        (owners, *groups),
        [pl.BlockSpec(memory_space=pltpu.SMEM)] + [on_chip()] * len(groups),
        (shape, shape),
        (on_chip(), on_chip()),
        0,
        name,
    )


def placement():
    me = lax.axis_index("col")
    high, z, core = me // 8, (me // 2) % 4, me % 2
    out = []
    for q in (0, 1):
        for k, s in enumerate(STEPS):
            for h in (0, 1):
                x = high if h == 0 else 1 - high
                c = core if q == 0 else 1 - core
                out.append((4 * q + k, (h,), x * 8 + ((z + 4 - s) % 4) * 2 + c))
    return out


def spread(pair):
    return [pair] + [moved(pair, route(0, s)) for s in STEPS[1:]]


def both_cores(arrays):
    return arrays + [moved(a, lambda i: i ^ 1) for a in arrays]


def split(value):
    hi = value.astype(jnp.bfloat16)
    return hi, (value - hi.astype(jnp.float32)).astype(jnp.bfloat16)


def times(hi, lo, value):
    v_hi, v_lo = split(value)
    total = jnp.dot(hi, v_lo, preferred_element_type=jnp.float32)
    total += jnp.dot(lo, v_hi, preferred_element_type=jnp.float32)
    return total + jnp.dot(hi, v_hi, preferred_element_type=jnp.float32)


def work(windows, width):
    return windows * 3 * 2 * F * F * width


def strip_shapes(width):
    rows = (HALF, F, HALF)
    return tuple(jax.ShapeDtypeStruct((r, width), jnp.float32) for r in rows)


def tiles(width):
    return [slice(t, t + TILE) for t in range(0, width, TILE)]


def round0(strip, first, width, hi, lo):
    def body(x_ref, hi_ref, lo_ref, h0_ref, h12_ref, h3_ref, held, sems):
        copies = {}
        for t, part in enumerate(tiles(width)):
            for s in (0, 1):
                copies[t, s] = pltpu.make_async_copy(
                    x_ref.at[s * F : (s + 1) * F, first + part.start : first + part.stop],
                    held.at[t, s],
                    sems.at[t, s],
                )
                copies[t, s].start()
        for t, part in enumerate(tiles(width)):
            copies[t, 0].wait()
            s0 = times(hi_ref[0], lo_ref[0], held[t, 0])
            h0_ref[:, part] = s0[:HALF]
            h12_ref[:HALF, part] = s0[HALF:]
            copies[t, 1].wait()
            s1 = times(hi_ref[1], lo_ref[1], held[t, 1])
            h12_ref[HALF:, part] = s1[:HALF]
            h3_ref[:, part] = s1[HALF:]

    count = len(tiles(width))
    return kernel(
        body,
        (strip, hi, lo),
        [pl.BlockSpec(memory_space=pltpu.HBM), on_chip(), on_chip()],
        strip_shapes(width),
        (on_chip(),) * 3,
        work(2, width),
        "round0",
        [pltpu.VMEM((count, 2, F, TILE), jnp.float32), pltpu.SemaphoreType.DMA((count, 2))],
    )


def odd(above, h0, h12, h3, below, hi, lo):
    middle = times(hi[1], lo[1], h12)
    top = times(hi[0, HALF:, :HALF], lo[0, HALF:, :HALF], above)
    top += times(hi[0, HALF:, HALF:], lo[0, HALF:, HALF:], h0)
    bottom = times(hi[2, :HALF, :HALF], lo[2, :HALF, :HALF], h3)
    bottom += times(hi[2, :HALF, HALF:], lo[2, :HALF, HALF:], below)
    return top, middle, bottom


def rounds12(above, h0, h12, h3, below, hi, lo, outer=None):
    width = h0.shape[1]
    outer = outer or ()

    def body(a_ref, h0_ref, h12_ref, h3_ref, f_ref, hi_ref, lo_ref, *rest):
        o0, o12, o3 = rest[-3:]
        for part in tiles(width):
            a, f = a_ref[:, part], f_ref[:, part]
            if outer:
                out_hi, out_lo = rest[:2]
                a = times(out_hi[1, HALF:], out_lo[1, HALF:], a)
                f = times(out_hi[2, :HALF], out_lo[2, :HALF], f)
            top, middle, bottom = odd(
                a, h0_ref[:, part], h12_ref[:, part], h3_ref[:, part], f, hi_ref, lo_ref
            )
            s0 = times(hi_ref[3], lo_ref[3], jnp.concatenate([top, middle[:HALF]], 0))
            o0[:, part] = s0[:HALF]
            o12[:HALF, part] = s0[HALF:]
            s1 = times(hi_ref[4], lo_ref[4], jnp.concatenate([middle[HALF:], bottom], 0))
            o12[HALF:, part] = s1[:HALF]
            o3[:, part] = s1[HALF:]

    args = (above, h0, h12, h3, below, hi, lo, *outer)
    return kernel(
        body,
        args,
        [on_chip()] * len(args),
        strip_shapes(width),
        (on_chip(),) * 3,
        work(5 if outer else 4, width),
        "rounds12",
    )


def round3(above, h0, h12, h3, below, hi, lo, at, result, first, columns):
    width = h0.shape[1]

    def body(a_ref, h0_ref, h12_ref, h3_ref, f_ref, hi_ref, lo_ref, *rest):
        out, held, sems = rest[-3:]
        copies = []
        for t, part in enumerate(tiles(width)):
            parts = odd(
                a_ref[:, part],
                h0_ref[:, part],
                h12_ref[:, part],
                h3_ref[:, part],
                f_ref[:, part],
                hi_ref,
                lo_ref,
            )
            row = 0
            for p, value in enumerate(parts):
                rows = slice(row, row + value.shape[0])
                held[t, rows] = value
                copies.append(
                    pltpu.make_async_copy(
                        held.at[t, rows],
                        out.at[rows, first + part.start : first + part.stop],
                        sems.at[t, p],
                    )
                )
                copies[-1].start()
                row = rows.stop
        for copy in copies:
            copy.wait()

    args = [above, h0, h12, h3, below, hi, lo]
    specs = [on_chip()] * len(args)
    aliases = {}
    if result is not None:
        aliases = {len(args): 0}
        args.append(result)
        specs.append(pl.BlockSpec(memory_space=pltpu.HBM))
    count = len(tiles(width))
    return kernel(
        body,
        args,
        specs,
        jax.ShapeDtypeStruct((2 * F, columns), jnp.float32),
        pl.BlockSpec(memory_space=pltpu.HBM),
        work(2, width),
        "round3",
        [pltpu.VMEM((count, 2 * F, TILE), jnp.float32), pltpu.SemaphoreType.DMA((count, 3))],
        aliases,
    )


def exchanged(strip):
    h0, _, h3 = strip
    return shifted(h3, 1), shifted(h0, -1)


def after(value, *others):
    return lax.optimization_barrier((value, others))[0]


def local(matrix_rows, factor_bank, owner_table):
    columns = matrix_rows.shape[1]
    strip = pltpu.with_memory_space_constraint(matrix_rows, pltpu.HBM)
    beside = moved(factor_bank, route(1, 0))
    early = spread(jnp.stack([factor_bank[0], beside[0]]))
    places = jnp.pad(owner_table[:, 0].astype(jnp.float32), ((0, 4), (0, F - 16)))
    firsts = [bank[r, 0] for bank in (factor_bank, beside) for r in (1, 3)]
    following = shifted(jnp.concatenate(firsts + [places], 0), -1)
    next_owner = following[128:132, :16].astype(jnp.int32)
    following = following[:128].reshape(2, 2, 32, F)
    banks = tuple(zip((factor_bank, beside), following))
    mid = [jnp.concatenate([bank[1], new[:1], bank[2]], 0) for bank, new in banks]
    mid = spread(after(jnp.stack(mid), early[1]))
    late = [jnp.concatenate([bank[3], new[1:]], 0) for bank, new in banks]
    late = spread(after(jnp.stack(late), mid))

    hi0, lo0 = prep(both_cores(early), placement, owner_table[0], "place0")
    strips, halos = [], []
    for c, (first, width) in enumerate(CHUNKS):
        order = after(hi0, strips[-1][0]) if c else hi0
        order = after(order, halos[c - 2]) if c > 1 else order
        strips.append(round0(strip, first, width, order, lo0))
        halos.append(exchanged(strips[-1]))
    mid = both_cores(list(after(mid, strips[1], halos[0])))
    owners = jnp.concatenate([owner_table[1], next_owner[1:2], owner_table[2]], 0)
    hi12, lo12 = prep(mid, placement, owners, "place12")
    ready = list(halos)
    for c, (a, f) in enumerate(ready):
        order = after(hi12, strips[c - 1][0], ready[2]) if c else after(hi12, ready[1])
        order = after(order, halos[c - 2]) if c > 1 else order
        strips[c] = rounds12(a, *strips[c], f, order, lo12)
        halos[c] = exchanged(strips[c])
    late = both_cores(list(after(late, strips[1])))
    owners = jnp.concatenate([owner_table[3], next_owner[3:]], 0)
    hi3, lo3 = prep(late, placement, owners, "place3")
    result = None
    for (first, _), (h0, h12, h3), (a, f) in zip(CHUNKS, strips, halos):
        result = round3(a, h0, h12, h3, f, hi3, lo3, (0, 1, 2), result, first, columns)
    return result


def solution(mesh):
    in_specs = (P("sec", "col"), P(None, "sec", "col", None), P(None, "sec", None))
    out_specs = P("sec", "col")
    return jax.shard_map(local, mesh=mesh, in_specs=in_specs, out_specs=out_specs, check_vma=False)
```

```python
import jax
import jax.numpy as jnp
from jax import lax
from jax.experimental import pallas as pl
from jax.experimental.pallas import tpu as pltpu
from jax.sharding import PartitionSpec as P

F = 512
HALF = 256
TILE = 512
COST = 0.01
CHUNKS = ((0, 1024), (1024, 512), (1536, 512))
VMEM = 16 * 1024 * 1024


def shifted(value, steps):
    count = lax.axis_size("sec")
    return lax.ppermute(value, "sec", [(i, (i + steps) % count) for i in range(count)])


def moved(value, target):
    return lax.ppermute(value, "col", [(i, target(i)) for i in range(16)])


def route(h, s):
    return lambda i: ((i // 8) ^ h) * 8 + ((i // 2 + s) % 4) * 2 + i % 2


STEPS = (0, 1, 3, 2)


def on_chip():
    return pl.BlockSpec(memory_space=pltpu.VMEM)


def kernel(body, args, in_specs, out_shapes, out_specs, flops, name, scratch=(), aliases=None):
    moved_bytes = sum(a.size * a.dtype.itemsize for a, b in zip(args, in_specs) if b.memory_space != pltpu.HBM)
    return pl.pallas_call(
        body,
        in_specs=in_specs,
        out_specs=out_specs,
        out_shape=out_shapes,
        scratch_shapes=scratch,
        input_output_aliases=aliases or {},
        compiler_params=pltpu.CompilerParams(vmem_limit_bytes=VMEM),
        cost_estimate=pl.CostEstimate(
            flops=int(COST * flops), bytes_accessed=int(COST * moved_bytes), transcendentals=0
        ),
        name=name,
    )(*args)


def prep(groups, index, owners, name, start=0):
    count = owners.shape[0]

    def body(owner_ref, *refs):
        ins, (hi_ref, lo_ref) = refs[: len(groups)], refs[len(groups) :]
        for array, at, source in index():
            for n in range(count):
                rows = pl.ds(pl.multiple_of(owner_ref[n, source] * 32, 32), 32)
                value = ins[array][at + (start + n,)]
                hi = value.astype(jnp.bfloat16)
                hi_ref[n, rows, :] = hi
                lo_ref[n, rows, :] = (value - hi.astype(jnp.float32)).astype(jnp.bfloat16)

    shape = jax.ShapeDtypeStruct((count, F, F), jnp.bfloat16)
    return kernel(
        body,
        (owners, *groups),
        [pl.BlockSpec(memory_space=pltpu.SMEM)] + [on_chip()] * len(groups),
        (shape, shape),
        (on_chip(), on_chip()),
        0,
        name,
    )


def placement():
    me = lax.axis_index("col")
    high, z, core = me // 8, (me // 2) % 4, me % 2
    out = []
    for q in (0, 1):
        for k, s in enumerate(STEPS):
            for h in (0, 1):
                x = high if h == 0 else 1 - high
                c = core if q == 0 else 1 - core
                out.append((4 * q + k, (h,), x * 8 + ((z + 4 - s) % 4) * 2 + c))
    return out


def spread(pair):
    return [pair] + [moved(pair, route(0, s)) for s in STEPS[1:]]


def both_cores(arrays):
    return arrays + [moved(a, lambda i: i ^ 1) for a in arrays]


def split(value):
    hi = value.astype(jnp.bfloat16)
    return hi, (value - hi.astype(jnp.float32)).astype(jnp.bfloat16)


def times(hi, lo, value):
    v_hi, v_lo = split(value)
    total = jnp.dot(hi, v_lo, preferred_element_type=jnp.float32)
    total += jnp.dot(lo, v_hi, preferred_element_type=jnp.float32)
    return total + jnp.dot(hi, v_hi, preferred_element_type=jnp.float32)


def work(windows, width):
    return windows * 3 * 2 * F * F * width


def strip_shapes(width):
    rows = (HALF, F, HALF)
    return tuple(jax.ShapeDtypeStruct((r, width), jnp.float32) for r in rows)


def tiles(width):
    return [slice(t, t + TILE) for t in range(0, width, TILE)]


def round0(strip, first, width, hi, lo):
    def body(x_ref, hi_ref, lo_ref, h0_ref, h12_ref, h3_ref, held, sems):
        copies = {}
        for t, part in enumerate(tiles(width)):
            for s in (0, 1):
                copies[t, s] = pltpu.make_async_copy(
                    x_ref.at[s * F : (s + 1) * F, first + part.start : first + part.stop],
                    held.at[t, s],
                    sems.at[t, s],
                )
                copies[t, s].start()
        for t, part in enumerate(tiles(width)):
            copies[t, 0].wait()
            s0 = times(hi_ref[0], lo_ref[0], held[t, 0])
            h0_ref[:, part] = s0[:HALF]
            h12_ref[:HALF, part] = s0[HALF:]
            copies[t, 1].wait()
            s1 = times(hi_ref[1], lo_ref[1], held[t, 1])
            h12_ref[HALF:, part] = s1[:HALF]
            h3_ref[:, part] = s1[HALF:]

    count = len(tiles(width))
    return kernel(
        body,
        (strip, hi, lo),
        [pl.BlockSpec(memory_space=pltpu.HBM), on_chip(), on_chip()],
        strip_shapes(width),
        (on_chip(),) * 3,
        work(2, width),
        "round0",
        [pltpu.VMEM((count, 2, F, TILE), jnp.float32), pltpu.SemaphoreType.DMA((count, 2))],
    )


def odd(above, h0, h12, h3, below, hi, lo):
    middle = times(hi[1], lo[1], h12)
    top = times(hi[0, HALF:, :HALF], lo[0, HALF:, :HALF], above)
    top += times(hi[0, HALF:, HALF:], lo[0, HALF:, HALF:], h0)
    bottom = times(hi[2, :HALF, :HALF], lo[2, :HALF, :HALF], h3)
    bottom += times(hi[2, :HALF, HALF:], lo[2, :HALF, HALF:], below)
    return top, middle, bottom


def rounds12(above, h0, h12, h3, below, hi, lo, outer=None):
    width = h0.shape[1]
    outer = outer or ()

    def body(a_ref, h0_ref, h12_ref, h3_ref, f_ref, hi_ref, lo_ref, *rest):
        o0, o12, o3 = rest[-3:]
        for part in tiles(width):
            a, f = a_ref[:, part], f_ref[:, part]
            if outer:
                out_hi, out_lo = rest[:2]
                a = times(out_hi[1, HALF:], out_lo[1, HALF:], a)
                f = times(out_hi[2, :HALF], out_lo[2, :HALF], f)
            top, middle, bottom = odd(
                a, h0_ref[:, part], h12_ref[:, part], h3_ref[:, part], f, hi_ref, lo_ref
            )
            s0 = times(hi_ref[3], lo_ref[3], jnp.concatenate([top, middle[:HALF]], 0))
            o0[:, part] = s0[:HALF]
            o12[:HALF, part] = s0[HALF:]
            s1 = times(hi_ref[4], lo_ref[4], jnp.concatenate([middle[HALF:], bottom], 0))
            o12[HALF:, part] = s1[:HALF]
            o3[:, part] = s1[HALF:]

    args = (above, h0, h12, h3, below, hi, lo, *outer)
    return kernel(
        body,
        args,
        [on_chip()] * len(args),
        strip_shapes(width),
        (on_chip(),) * 3,
        work(5 if outer else 4, width),
        "rounds12",
    )


def round3(above, h0, h12, h3, below, hi, lo, at, result, first, columns):
    width = h0.shape[1]

    def body(a_ref, h0_ref, h12_ref, h3_ref, f_ref, hi_ref, lo_ref, *rest):
        out, held, sems = rest[-3:]
        copies = []
        for t, part in enumerate(tiles(width)):
            parts = odd(
                a_ref[:, part],
                h0_ref[:, part],
                h12_ref[:, part],
                h3_ref[:, part],
                f_ref[:, part],
                hi_ref,
                lo_ref,
            )
            row = 0
            for p, value in enumerate(parts):
                rows = slice(row, row + value.shape[0])
                held[t, rows] = value
                copies.append(
                    pltpu.make_async_copy(
                        held.at[t, rows],
                        out.at[rows, first + part.start : first + part.stop],
                        sems.at[t, p],
                    )
                )
                copies[-1].start()
                row = rows.stop
        for copy in copies:
            copy.wait()

    args = [above, h0, h12, h3, below, hi, lo]
    specs = [on_chip()] * len(args)
    aliases = {}
    if result is not None:
        aliases = {len(args): 0}
        args.append(result)
        specs.append(pl.BlockSpec(memory_space=pltpu.HBM))
    count = len(tiles(width))
    return kernel(
        body,
        args,
        specs,
        jax.ShapeDtypeStruct((2 * F, columns), jnp.float32),
        pl.BlockSpec(memory_space=pltpu.HBM),
        work(2, width),
        "round3",
        [pltpu.VMEM((count, 2 * F, TILE), jnp.float32), pltpu.SemaphoreType.DMA((count, 3))],
        aliases,
    )


def exchanged(strip):
    h0, _, h3 = strip
    return shifted(h3, 1), shifted(h0, -1)


def after(value, *others):
    return lax.optimization_barrier((value, others))[0]


def local(matrix_rows, factor_bank, owner_table):
    columns = matrix_rows.shape[1]
    strip = pltpu.with_memory_space_constraint(matrix_rows, pltpu.HBM)
    pair = jnp.stack([factor_bank[0], moved(factor_bank[0], route(1, 0))])
    early = spread(pair)
    beside = moved(after(factor_bank[1:], pair), route(1, 0))
    places = jnp.pad(owner_table[:, 0].astype(jnp.float32), ((0, 4), (0, F - 16)))
    firsts = [bank[r, 0] for bank in (factor_bank[1:], beside) for r in (0, 2)]
    following = shifted(after(jnp.concatenate(firsts + [places], 0), early[3]), -1)
    next_owner = following[128:132, :16].astype(jnp.int32)
    following = following[:128].reshape(2, 2, 32, F)
    banks = tuple(zip((factor_bank[1:], beside), following))
    mid = [jnp.concatenate([bank[0], new[:1], bank[1]], 0) for bank, new in banks]
    late = [jnp.concatenate([bank[2], new[1:]], 0) for bank, new in banks]

    hi0, lo0 = prep(both_cores(early), placement, owner_table[0], "place0")
    strips, halos = [], []
    for c, (first, width) in enumerate(CHUNKS):
        order = after(hi0, strips[-1][0]) if c else hi0
        order = after(order, halos[c - 2]) if c > 1 else order
        strips.append(round0(strip, first, width, order, lo0))
        halos.append(exchanged(strips[-1]))
    mid = spread(jnp.stack(mid))
    late = spread(after(jnp.stack(late), mid))
    mid = both_cores(list(after(mid, strips[1], halos[0])))
    owners = jnp.concatenate([owner_table[1], next_owner[1:2], owner_table[2]], 0)
    hi12, lo12 = prep(mid, placement, owners, "place12")
    ready = list(halos)
    for c, (a, f) in enumerate(ready):
        order = after(hi12, strips[c - 1][0], ready[2]) if c else after(hi12, ready[1])
        order = after(order, halos[c - 2]) if c > 1 else order
        strips[c] = rounds12(a, *strips[c], f, order, lo12)
        halos[c] = exchanged(strips[c])
    late = both_cores(list(after(late, strips[1])))
    owners = jnp.concatenate([owner_table[3], next_owner[3:]], 0)
    hi3, lo3 = prep(late, placement, owners, "place3")
    result = None
    for (first, _), (h0, h12, h3), (a, f) in zip(CHUNKS, strips, halos):
        result = round3(a, h0, h12, h3, f, hi3, lo3, (0, 1, 2), result, first, columns)
    return result


def solution(mesh):
    in_specs = (P("sec", "col"), P(None, "sec", "col", None), P(None, "sec", None))
    out_specs = P("sec", "col")
    return jax.shard_map(local, mesh=mesh, in_specs=in_specs, out_specs=out_specs, check_vma=False)
```

```python
import jax
import jax.numpy as jnp
from jax import lax
from jax.experimental import pallas as pl
from jax.experimental.pallas import tpu as pltpu
from jax.sharding import PartitionSpec as P

F = 512
HALF = 256
TILE = 512
COST = 0.01
CHUNKS = ((0, 1024), (1024, 512), (1536, 512))
VMEM = 16 * 1024 * 1024


def shifted(value, steps):
    count = lax.axis_size("sec")
    return lax.ppermute(value, "sec", [(i, (i + steps) % count) for i in range(count)])


def moved(value, target):
    return lax.ppermute(value, "col", [(i, target(i)) for i in range(16)])


def route(h, s):
    return lambda i: ((i // 8) ^ h) * 8 + ((i // 2 + s) % 4) * 2 + i % 2


STEPS = (0, 1, 3, 2)


def on_chip():
    return pl.BlockSpec(memory_space=pltpu.VMEM)


def kernel(body, args, in_specs, out_shapes, out_specs, flops, name, scratch=(), aliases=None):
    moved_bytes = sum(a.size * a.dtype.itemsize for a, b in zip(args, in_specs) if b.memory_space != pltpu.HBM)
    return pl.pallas_call(
        body,
        in_specs=in_specs,
        out_specs=out_specs,
        out_shape=out_shapes,
        scratch_shapes=scratch,
        input_output_aliases=aliases or {},
        compiler_params=pltpu.CompilerParams(vmem_limit_bytes=VMEM),
        cost_estimate=pl.CostEstimate(
            flops=int(COST * flops), bytes_accessed=int(COST * moved_bytes), transcendentals=0
        ),
        name=name,
    )(*args)


def prep(groups, index, owners, name, start=0):
    count = owners.shape[0]

    def body(owner_ref, *refs):
        ins, (hi_ref, lo_ref) = refs[: len(groups)], refs[len(groups) :]
        for array, at, source in index():
            for n in range(count):
                rows = pl.ds(pl.multiple_of(owner_ref[n, source] * 32, 32), 32)
                value = ins[array][at + (start + n,)]
                hi = value.astype(jnp.bfloat16)
                hi_ref[n, rows, :] = hi
                lo_ref[n, rows, :] = (value - hi.astype(jnp.float32)).astype(jnp.bfloat16)

    shape = jax.ShapeDtypeStruct((count, F, F), jnp.bfloat16)
    return kernel(
        body,
        (owners, *groups),
        [pl.BlockSpec(memory_space=pltpu.SMEM)] + [on_chip()] * len(groups),
        (shape, shape),
        (on_chip(), on_chip()),
        0,
        name,
    )


def placement():
    me = lax.axis_index("col")
    high, z, core = me // 8, (me // 2) % 4, me % 2
    out = []
    for q in (0, 1):
        for k, s in enumerate(STEPS):
            for h in (0, 1):
                x = high if h == 0 else 1 - high
                c = core if q == 0 else 1 - core
                out.append((4 * q + k, (h,), x * 8 + ((z + 4 - s) % 4) * 2 + c))
    return out


def spread(pair):
    return [pair] + [moved(pair, route(0, s)) for s in STEPS[1:]]


def both_cores(arrays):
    return arrays + [moved(a, lambda i: i ^ 1) for a in arrays]


def split(value):
    hi = value.astype(jnp.bfloat16)
    return hi, (value - hi.astype(jnp.float32)).astype(jnp.bfloat16)


def times(hi, lo, value):
    v_hi, v_lo = split(value)
    total = jnp.dot(hi, v_lo, preferred_element_type=jnp.float32)
    total += jnp.dot(lo, v_hi, preferred_element_type=jnp.float32)
    return total + jnp.dot(hi, v_hi, preferred_element_type=jnp.float32)


def work(windows, width):
    return windows * 3 * 2 * F * F * width


def strip_shapes(width):
    rows = (HALF, F, HALF)
    return tuple(jax.ShapeDtypeStruct((r, width), jnp.float32) for r in rows)


def tiles(width):
    return [slice(t, t + TILE) for t in range(0, width, TILE)]


def round0(strip, first, width, hi, lo):
    def body(x_ref, hi_ref, lo_ref, h0_ref, h12_ref, h3_ref, held, sems):
        copies = {}
        for t, part in enumerate(tiles(width)):
            for s in (0, 1):
                copies[t, s] = pltpu.make_async_copy(
                    x_ref.at[s * F : (s + 1) * F, first + part.start : first + part.stop],
                    held.at[t, s],
                    sems.at[t, s],
                )
                copies[t, s].start()
        for t, part in enumerate(tiles(width)):
            copies[t, 0].wait()
            s0 = times(hi_ref[0], lo_ref[0], held[t, 0])
            h0_ref[:, part] = s0[:HALF]
            h12_ref[:HALF, part] = s0[HALF:]
            copies[t, 1].wait()
            s1 = times(hi_ref[1], lo_ref[1], held[t, 1])
            h12_ref[HALF:, part] = s1[:HALF]
            h3_ref[:, part] = s1[HALF:]

    count = len(tiles(width))
    return kernel(
        body,
        (strip, hi, lo),
        [pl.BlockSpec(memory_space=pltpu.HBM), on_chip(), on_chip()],
        strip_shapes(width),
        (on_chip(),) * 3,
        work(2, width),
        "round0",
        [pltpu.VMEM((count, 2, F, TILE), jnp.float32), pltpu.SemaphoreType.DMA((count, 2))],
    )


def odd(above, h0, h12, h3, below, hi, lo):
    middle = times(hi[1], lo[1], h12)
    top = times(hi[0, HALF:, :HALF], lo[0, HALF:, :HALF], above)
    top += times(hi[0, HALF:, HALF:], lo[0, HALF:, HALF:], h0)
    bottom = times(hi[2, :HALF, :HALF], lo[2, :HALF, :HALF], h3)
    bottom += times(hi[2, :HALF, HALF:], lo[2, :HALF, HALF:], below)
    return top, middle, bottom


def rounds12(above, h0, h12, h3, below, hi, lo, outer=None):
    width = h0.shape[1]
    outer = outer or ()

    def body(a_ref, h0_ref, h12_ref, h3_ref, f_ref, hi_ref, lo_ref, *rest):
        o0, o12, o3 = rest[-3:]
        for part in tiles(width):
            a, f = a_ref[:, part], f_ref[:, part]
            if outer:
                out_hi, out_lo = rest[:2]
                a = times(out_hi[1, HALF:], out_lo[1, HALF:], a)
                f = times(out_hi[2, :HALF], out_lo[2, :HALF], f)
            top, middle, bottom = odd(
                a, h0_ref[:, part], h12_ref[:, part], h3_ref[:, part], f, hi_ref, lo_ref
            )
            s0 = times(hi_ref[3], lo_ref[3], jnp.concatenate([top, middle[:HALF]], 0))
            o0[:, part] = s0[:HALF]
            o12[:HALF, part] = s0[HALF:]
            s1 = times(hi_ref[4], lo_ref[4], jnp.concatenate([middle[HALF:], bottom], 0))
            o12[HALF:, part] = s1[:HALF]
            o3[:, part] = s1[HALF:]

    args = (above, h0, h12, h3, below, hi, lo, *outer)
    return kernel(
        body,
        args,
        [on_chip()] * len(args),
        strip_shapes(width),
        (on_chip(),) * 3,
        work(5 if outer else 4, width),
        "rounds12",
    )


def round3(above, h0, h12, h3, below, hi, lo, at, result, first, columns):
    width = h0.shape[1]

    def body(a_ref, h0_ref, h12_ref, h3_ref, f_ref, hi_ref, lo_ref, *rest):
        out, held, sems = rest[-3:]
        copies = []
        for t, part in enumerate(tiles(width)):
            parts = odd(
                a_ref[:, part],
                h0_ref[:, part],
                h12_ref[:, part],
                h3_ref[:, part],
                f_ref[:, part],
                hi_ref,
                lo_ref,
            )
            row = 0
            for p, value in enumerate(parts):
                rows = slice(row, row + value.shape[0])
                held[t, rows] = value
                copies.append(
                    pltpu.make_async_copy(
                        held.at[t, rows],
                        out.at[rows, first + part.start : first + part.stop],
                        sems.at[t, p],
                    )
                )
                copies[-1].start()
                row = rows.stop
        for copy in copies:
            copy.wait()

    args = [above, h0, h12, h3, below, hi, lo]
    specs = [on_chip()] * len(args)
    aliases = {}
    if result is not None:
        aliases = {len(args): 0}
        args.append(result)
        specs.append(pl.BlockSpec(memory_space=pltpu.HBM))
    count = len(tiles(width))
    return kernel(
        body,
        args,
        specs,
        jax.ShapeDtypeStruct((2 * F, columns), jnp.float32),
        pl.BlockSpec(memory_space=pltpu.HBM),
        work(2, width),
        "round3",
        [pltpu.VMEM((count, 2 * F, TILE), jnp.float32), pltpu.SemaphoreType.DMA((count, 3))],
        aliases,
    )


def exchanged(strip):
    h0, _, h3 = strip
    return shifted(h3, 1), shifted(h0, -1)


def after(value, *others):
    return lax.optimization_barrier((value, others))[0]


def local(matrix_rows, factor_bank, owner_table):
    columns = matrix_rows.shape[1]
    strip = pltpu.with_memory_space_constraint(matrix_rows, pltpu.HBM)
    pair = jnp.stack([factor_bank[0], moved(factor_bank[0], route(1, 0))])
    early = spread(pair)
    beside = moved(after(factor_bank[1:], pair), route(1, 0))
    places = jnp.pad(owner_table[:, 0].astype(jnp.float32), ((0, 4), (0, F - 16)))
    firsts = [bank[r, 0] for bank in (factor_bank[1:], beside) for r in (0, 2)]
    following = shifted(after(jnp.concatenate(firsts + [places], 0), early[3]), -1)
    next_owner = following[128:132, :16].astype(jnp.int32)
    following = following[:128].reshape(2, 2, 32, F)
    banks = tuple(zip((factor_bank[1:], beside), following))
    mid = [jnp.concatenate([bank[0], new[:1], bank[1]], 0) for bank, new in banks]
    late = [jnp.concatenate([bank[2], new[1:]], 0) for bank, new in banks]

    hi0, lo0 = prep(both_cores(early), placement, owner_table[0], "place0")
    strips, halos = [], []
    for c, (first, width) in enumerate(CHUNKS):
        order = after(hi0, strips[-1][0]) if c else hi0
        order = after(order, halos[c - 2]) if c > 1 else order
        strips.append(round0(strip, first, width, order, lo0))
        halos.append(exchanged(strips[-1]))
    mid = spread(jnp.stack(mid))
    late = spread(after(jnp.stack(late), mid))
    mid = both_cores(list(after(mid, strips[1], halos[0])))
    owners = jnp.concatenate([owner_table[1], next_owner[1:2], owner_table[2]], 0)
    hi12, lo12 = prep(mid, placement, owners, "place12")
    ready = list(halos)
    for c, (a, f) in enumerate(ready):
        order = after(hi12, strips[c - 1][0], ready[2]) if c else after(hi12, ready[1])
        order = after(order, halos[c - 2]) if c > 1 else order
        strips[c] = rounds12(a, *strips[c], f, order, lo12)
        halos[c] = exchanged(strips[c])
    late = both_cores(list(after(late, strips[0][0])))
    owners = jnp.concatenate([owner_table[3], next_owner[3:]], 0)
    hi3, lo3 = prep(late, placement, owners, "place3")
    result = None
    for (first, _), (h0, h12, h3), (a, f) in zip(CHUNKS, strips, halos):
        result = round3(a, h0, h12, h3, f, hi3, lo3, (0, 1, 2), result, first, columns)
    return result


def solution(mesh):
    in_specs = (P("sec", "col"), P(None, "sec", "col", None), P(None, "sec", None))
    out_specs = P("sec", "col")
    return jax.shard_map(local, mesh=mesh, in_specs=in_specs, out_specs=out_specs, check_vma=False)
```
